1024 devices in a mesh: fsdp: 32 (over x_lo, z, core), adapter: 32 (over x_hi, y).
Axes of the slice: x: 8 (x_hi: 4, x_lo: 2; x = x_hi * 2 + x_lo), y: 8, z: 8, core: 2. Of those that a mesh axis runs over, the one named last changes fastest.
Arguments:
- tokens: bfloat16 [131072, 6144], P(('fsdp', 'adapter')), may hold values from -6 to 6
- route_ids: int32 [131072, 2], P(('fsdp', 'adapter')), may hold values from 0 to 31, all different within a row; in each aligned block of 64 rows (0 to 63, 64 to 127, ...) at most 5 rows name the same one
- router_weight: bfloat16 [6144, 32], replicated, may hold values from -0.078125 to 0.078125
- adapter_down: bfloat16 [32, 6144, 32], P('adapter'), may hold values from -0.078125 to 0.078125
- adapter_up: bfloat16 [32, 32, 6144], P('adapter'), may hold values from -1 to 1
- norm_gain: float32 [6144], replicated, may hold values from 0.5 to 1.5
- frozen_weight: bfloat16 [6144, 512], P('fsdp'), may hold values from -0.078125 to 0.078125
Outputs:
- residual: bfloat16 [131072, 6144], P(('fsdp', 'adapter'))
- projected: bfloat16 [131072, 512], P(('fsdp', 'adapter'))
The draws below stay inside these ranges and needn't reach their ends.
Inputs may be any that keep to these rules, and one draw needn't show every extreme that they name: `route_ids`: each row names two different adapter experts. Within each aligned block of 64 rows, no expert is named more than 5 times, a bound that some block reaches.
All inputs are finite; a program needn't handle non-finite values.
Results may differ from the reference program's by a relative error of at most 0.0056.
Values may be sent and summed in bfloat16 or wider, within the bound.
A program may use at most 64 MiB of HBM per device.

```python
import math
import jax
import jax.numpy as jnp
import numpy as np
from jax import lax

D = 6144
KV = 512
R = 32
HALF = 64
EXPERTS = 32
CAP = 5
TOKENS = 131072


def levels(key, extent, pieces, smallest, top_value):
    def one(dim, blocks):
        draws = jax.random.uniform(jax.random.fold_in(jax.random.fold_in(key, 6), dim), (blocks,), jnp.float32, smallest / len(pieces), top_value / len(pieces))
        return jnp.repeat(jnp.exp(draws), extent[dim] // blocks).reshape((-1,) + (1,) * (len(extent) - dim - 1))

    loudness = one(*pieces[0])
    for cut in pieces[1:]:
        loudness = loudness * one(*cut)
    return loudness


def routed_block(own_key, own, number, rows, number_of, top, bound, lean):
    ranking = jax.random.permutation(own_key, number_of)
    heavy_load, ordinary = load_shares(number_of, rows * top, bound, lean, True), load_shares(number_of, rows * top, bound, lean, False)
    places = jnp.arange(number_of)

    def named(sizes, offset_by):
        used = int((sizes > 0).sum())
        fixed = max(1, used // 4)
        passed = fixed + (places - fixed + offset_by * (used - fixed)) % max(1, number_of - fixed)
        return jnp.zeros((number_of,), jnp.int32).at[ranking[jnp.where(places < fixed, places, passed)]].set(jnp.asarray(sizes, jnp.int32))

    sizes = jnp.where(number % 4 == 0, named(heavy_load, number // 4), named(ordinary, number - number // 4 - 1))
    mixed = jax.random.permutation(jax.random.fold_in(own, 3), number_of)
    donor, taker = mixed[0:number_of // 2 * 2:2], mixed[1:number_of // 2 * 2:2]
    room = jnp.minimum(sizes[donor] - 1, bound - sizes[taker]) // 2
    room = jnp.where((donor == ranking[0]) | (taker == ranking[0]) | (sizes[taker] == 0), 0, jnp.maximum(room, 0))
    passed = jax.random.randint(jax.random.fold_in(own, 4), (number_of // 2,), 0, 1 << 20) % (room + 1)
    sizes = sizes.at[donor].add(-passed).at[taker].add(passed)
    labels = jnp.searchsorted(jnp.cumsum(sizes), jnp.arange(rows * top), side="right").astype(jnp.int32)
    listing = labels.reshape(top, rows).T
    listing = listing[jax.random.permutation(jax.random.fold_in(own, 1), rows)]
    offset_by = jax.random.randint(jax.random.fold_in(own, 2), (rows, 1), 0, top)
    return jnp.take_along_axis(listing, (jnp.arange(top)[None, :] + offset_by) % top, axis=1)


def load_shares(number_of, total, reach, lean, full):
    loads = [(1 << 20) // math.isqrt(rank ** lean) + 1 for rank in range(1, number_of + 1)]
    largest = reach if full else min(reach, max(-(-total // number_of), total * loads[0] // sum(loads)))
    least = 1 if total - largest >= number_of - 1 else 0
    counts, spare = [largest] + [least] * (number_of - 1), total - largest - least * (number_of - 1)
    while spare > 0:
        movable = [i for i in range(1, number_of) if counts[i] < largest] or [i for i in range(1, number_of) if counts[i] < reach]
        mass, budget = sum([loads[i] for i in movable]), spare
        for i in movable:
            addition = min(reach - counts[i], max(1, budget * loads[i] // mass), spare)
            counts[i] = counts[i] + addition
            spare = spare - addition
    return np.array(counts)


def centred(rng, extent, scale, limit, shards=(), held_as=jnp.bfloat16):
    result = scale * jax.random.normal(rng, extent, jnp.float32)
    if shards:
        result = result * levels(rng, extent, shards, -0.22, 0.18)
    return jnp.clip(result, -limit, limit).astype(held_as)


def setup_inputs(seed: int = 0) -> dict:
    splits = jax.random.split(jax.random.key(seed), 8)
    tokens = centred(splits[0], (TOKENS, D), 1.0, 6.0, ((0, 1024),))
    route_ids_keys = jax.random.split(jax.random.fold_in(splits[1], 1), TOKENS // HALF)
    route_ids_turns = jax.random.permutation(jax.random.fold_in(splits[1], 3), TOKENS // HALF)
    route_ids = jax.vmap(lambda own, number: routed_block(jax.random.fold_in(splits[1], 2), own, number, HALF, EXPERTS, 2, CAP, 2))(route_ids_keys, route_ids_turns).reshape((TOKENS, 2))
    router_weight = centred(splits[2], (D, EXPERTS), D ** -0.5, 0.078125)
    adapter_down = centred(splits[3], (EXPERTS, D, R), D ** -0.5, 0.078125, ((0, 32),))
    adapter_up = centred(splits[4], (EXPERTS, R, D), R ** -0.5, 1.0, ((0, 32),))
    norm_gain = jnp.clip(1.0 + 0.1 * jax.random.normal(splits[5], (D,), jnp.float32), 0.5, 1.5)
    frozen_weight = centred(splits[6], (D, KV), D ** -0.5, 0.078125, ((0, 32),))
    return {"tokens": tokens, "route_ids": route_ids, "router_weight": router_weight, "adapter_down": adapter_down, "adapter_up": adapter_up, "norm_gain": norm_gain, "frozen_weight": frozen_weight}


def reference(tokens, route_ids, router_weight, adapter_down, adapter_up, norm_gain, frozen_weight):
    logits = jnp.dot(tokens, router_weight, preferred_element_type=jnp.float32)
    chosen = jnp.take_along_axis(logits, route_ids, axis=1)
    leading = jax.nn.sigmoid(chosen[:, 0] - chosen[:, 1])
    gate_pair = jnp.stack([leading, 1.0 - leading], axis=1)
    count = adapter_down.shape[0]

    def expert_step(running, packed):
        expert, down_map, up_map = packed
        weight = lax.optimization_barrier(jnp.sum(jnp.where(route_ids == expert, gate_pair, jnp.float32(0.0)), axis=1))
        low_rank = jnp.dot(tokens, down_map, preferred_element_type=jnp.float32).astype(jnp.bfloat16)
        delta = jnp.dot(low_rank, up_map, preferred_element_type=jnp.float32).astype(jnp.bfloat16)
        delta = lax.optimization_barrier(delta).astype(jnp.float32)
        return (running + weight[:, None] * delta, None)
    start = jnp.zeros(tokens.shape, jnp.float32)
    summed, _ = lax.scan(expert_step, start, (jnp.arange(count, dtype=jnp.int32), adapter_down, adapter_up))
    combined = tokens.astype(jnp.float32) + summed
    residual = combined.astype(jnp.bfloat16)
    scale = lax.rsqrt(lax.optimization_barrier(jnp.mean(combined * combined, axis=1, keepdims=True)) + 1e-05)
    normed = (combined * scale * norm_gain[None, :]).astype(jnp.bfloat16)
    projected = jnp.dot(normed, frozen_weight, preferred_element_type=jnp.float32).astype(jnp.bfloat16)
    return (residual, projected)
```

```python
import functools

import jax
import jax.numpy as jnp
from jax import lax
from jax.experimental import pallas as pl
from jax.experimental.pallas import tpu as pltpu
from jax.sharding import PartitionSpec as P

MESH = pl.DeviceIdType.MESH
NX, NY, NZ = 8, 8, 8
CHAINS = ((0, 1, 4), (1, 1, 3), (0, -1, 3), (1, -1, 4))
CHUNK = 256


def mult(value, of):
    return pl.multiple_of(value, of)


def flip(bit, by):
    return bit + by * (1 - 2 * bit)


def kernel(
    tok, code, down, up, router, frozen, gain, res, proj,
    X, CODE, DN, UP, RT, FZ, ACC0, ACC1, ACCR, P1, PIN, TS, TIN, A, RB, PB, PIN2,
    tok_s, tok_r, code_s, code_r, xd_s, xd_r, xu_s, xu_r, yd_s, yd_r, yu_s, yu_r,
    fz_s, fz_r, p1_s, p1_r, t_s, t_r, rb_s, rb_r, p2_s, p2_r, rt_sem,
):
    half = tok.shape[0] // 2
    width = X.shape[1]
    rank = down.shape[0]
    block = 4 * rank
    per_class = width // frozen.shape[0]
    fs, ad = lax.axis_index("fsdp"), lax.axis_index("adapter")
    x_lo = lax.div(fs, 2 * NZ)
    z = lax.rem(lax.div(fs, 2), NZ)
    core = lax.rem(fs, 2)
    x_hi = lax.div(ad, NY)
    y = lax.rem(ad, NY)
    x = 2 * x_hi + x_lo
    zb = lax.rem(z, 2)
    mine = x_lo * 4 + zb * 2 + core

    def dev(px, py, pz, pc):
        return (lax.rem(px, 2) * (2 * NZ) + pz * 2 + pc, lax.div(px, 2) * NY + py)

    def partner(h, d):
        px, pz, pc = x, z, core
        if d & 4:
            px = x + 1 - 2 * x_lo if h == 0 else lax.rem(x + NX - 1 + 2 * x_lo, NX)
        if d & 2:
            pz = z + 1 - 2 * zb if h == 0 else lax.rem(z + NZ - 1 + 2 * zb, NZ)
        if d & 1:
            pc = 1 - core
        return dev(px, y, pz, pc)

    def member(d):
        return flip(x_lo, (d >> 2) & 1) * 4 + flip(zb, (d >> 1) & 1) * 2 + flip(core, d & 1)

    own_cols = pl.ds(mult(mine * width, 128), width)
    groups = [(h, d) for d in (6, 4, 2, 7, 5, 3, 1) for h in range(2)]

    def remote(src, dst, send, recv, device):
        return pltpu.make_async_remote_copy(
            src_ref=src, dst_ref=dst, send_sem=send, recv_sem=recv, device_id=device, device_id_type=MESH
        )

    def rows_of(h, d):
        return pl.ds((h * 8 + d) * half, half)

    def tok_copy(h, d):
        i = h * 8 + d
        cols = pl.ds(mult(member(d) * width, 128), width)
        src = tok.at[pl.ds(h * half, half), cols]
        return remote(src, X.at[rows_of(h, d)], tok_s.at[i], tok_r.at[i], partner(h, d))

    def code_copy(h, d):
        i = h * 8 + d
        src = code.at[pl.ds(h * half, half)]
        return remote(src, CODE.at[rows_of(h, d)], code_s.at[i], code_r.at[i], partner(h, d))

    def slot(py, px_hi):
        return pl.ds(mult(py * block + px_hi * rank, rank), rank)

    def x_copy(src, buf, send, recv, d):
        device = dev(2 * lax.rem(x_hi + d, 4) + x_lo, y, z, core)
        return remote(src.at[:, own_cols], buf.at[slot(y, x_hi)], send.at[d], recv.at[d], device)

    def y_copy(buf, send, recv, chain, s):
        part, way, _ = CHAINS[chain]
        origin = lax.rem(y + NY - way * (s - 1), NY)
        rows = pl.ds(mult(origin * block + part * (block // 2), block // 2), block // 2)
        device = dev(x, lax.rem(y + NY + way, NY), z, core)
        i = chain * 4 + s - 1
        return remote(buf.at[rows], buf.at[rows], send.at[i], recv.at[i], device)

    fz_class = lax.div(fs, per_class)
    fz_core = lax.rem(fz_class, 2)
    fz_zb = lax.rem(lax.div(fz_class, 2), 2)
    fz_rows = frozen.shape[0]
    fz_slot = pl.ds(mult(lax.rem(fs, per_class) * fz_rows, 16), fz_rows)
    fz_self = (fz_class == mine)

    def fz_dest(k):
        return dev(x, y, 2 * k + fz_zb, fz_core)

    def fz_other(k):
        return jnp.logical_not(jnp.logical_and(2 * k + fz_zb == z, fz_core == core))

    def fz_copy(k):
        return remote(frozen, FZ.at[fz_slot], fz_s.at[k], fz_r.at[lax.rem(fs, per_class)], fz_dest(k))

    barrier = pltpu.get_barrier_semaphore()

    def greet(device):
        pl.semaphore_signal(barrier, inc=1, device_id=device, device_id_type=MESH)

    for h, d in groups:
        greet(partner(h, d))
    for d in range(1, 4):
        greet(dev(2 * lax.rem(x_hi + d, 4) + x_lo, y, z, core))
    for way in (1, -1):
        greet(dev(x, lax.rem(y + NY + way, NY), z, core))
    for b in range(per_class):
        source = mine * per_class + b

        @pl.when(source != fs)
        def _():
            greet((source, ad))

    RT[...] = jnp.zeros_like(RT)
    pl.semaphore_wait(barrier, 14 + 3 + 2 + NZ // 2 - fz_self.astype(jnp.int32))

    for src, buf, send, recv in ((down, DN, xd_s, xd_r),):
        for d in (2, 1, 3):
            x_copy(src, buf, send, recv, d).start()
        pltpu.make_async_copy(src.at[:, own_cols], buf.at[slot(y, x_hi)], recv.at[0]).start()
    for h, d in groups:
        code_copy(h, d).start()
        tok_copy(h, d).start()

    def tok_local(h):
        cp = pltpu.make_async_copy(tok.at[pl.ds(h * half, half), own_cols], X.at[rows_of(h, 0)], tok_r.at[h * 8])
        cq = pltpu.make_async_copy(code.at[pl.ds(h * half, half)], CODE.at[rows_of(h, 0)], code_r.at[h * 8])
        return cp, cq

    for h in range(2):
        for c in tok_local(h):
            c.start()
    rt_copy = pltpu.make_async_copy(router.at[:, own_cols], RT.at[pl.ds(2 * rank, rank)], rt_sem.at[0])
    rt_copy.start()

    def x_wait(src, buf, send, recv):
        pltpu.make_async_copy(src.at[:, own_cols], buf.at[slot(y, x_hi)], recv.at[0]).wait()
        for d in (1, 3, 2):
            x_copy(src, buf, send, recv, d).wait_recv()

    x_wait(down, DN, xd_s, xd_r)
    for c in range(4):
        y_copy(DN, yd_s, yd_r, c, 1).start()
    for d in (2, 1, 3):
        x_copy(up, UP, xu_s, xu_r, d).start()
    pltpu.make_async_copy(up.at[:, own_cols], UP.at[slot(y, x_hi)], xu_r.at[0]).start()

    for h in range(2):
        for c in tok_local(h):
            c.wait()
    for h, d in groups:
        code_copy(h, d).wait_recv()
        tok_copy(h, d).wait_recv()
    rt_copy.wait()

    total = X.shape[0]
    lane = lax.broadcasted_iota(jnp.int32, (CHUNK, 128), 1)
    group8 = (lane >> 5) * 8
    nt = (((1,), (1,)), ((), ()))

    def low_rank(py, first=False):
        def body(i, carry):
            rows = pl.ds(mult(i * CHUNK, CHUNK), CHUNK)
            xs = X[rows, :]
            got = lax.dot_general(
                xs, DN[pl.ds(mult(py * block, block), block), :], nt, preferred_element_type=jnp.float32
            )
            c = CODE[rows, :]
            id0, id1 = c >> 5, c & 31
            named = group8 + py
            part0 = jnp.where(id0 == named, got, 0.0)
            part1 = jnp.where(id1 == named, got, 0.0)
            if first:
                ACC0[rows, :] = part0
                ACC1[rows, :] = part1
                logit = lax.dot_general(xs, RT[...], nt, preferred_element_type=jnp.float32)
                at = lane - 64
                ACCR[rows, :] = jnp.where(at == id0, logit, 0.0) - jnp.where(at == id1, logit, 0.0)
            else:
                ACC0[rows, :] += part0
                ACC1[rows, :] += part1
            return carry

        lax.fori_loop(0, total // CHUNK, body, 0)

    def ring_step(buf, send, recv, s):
        for c in (0, 3, 1, 2):
            if s <= CHAINS[c][2]:
                y_copy(buf, send, recv, c, s).wait_recv()
                if s < CHAINS[c][2]:
                    y_copy(buf, send, recv, c, s + 1).start()

    low_rank(y, True)
    for s in range(1, 5):
        ring_step(DN, yd_s, yd_r, s)
        if s == 1:
            for k in range(NZ // 2):
                @pl.when(fz_other(k))
                def _():
                    fz_copy(k).start()

            @pl.when(fz_self)
            def _():
                pltpu.make_async_copy(frozen, FZ.at[fz_slot], fz_r.at[lax.rem(fs, per_class)]).start()
        if s == 3:
            x_wait(up, UP, xu_s, xu_r)
            for c in range(4):
                y_copy(UP, yu_s, yu_r, c, 1).start()
        low_rank(lax.rem(y + NY - s, NY))
        if s < 4:
            low_rank(lax.rem(y + s, NY))

    def pack(i, carry):
        rows = pl.ds(mult(i * CHUNK, CHUNK), CHUNK)
        a0, a1 = ACC0[rows, :], ACC1[rows, :]
        a0 = a0 + pltpu.roll(a0, 64, 1)
        a0 = a0 + pltpu.roll(a0, 32, 1)
        a1 = a1 + pltpu.roll(a1, 64, 1)
        a1 = a1 + pltpu.roll(a1, 32, 1)
        low = jnp.where(lane < 32, a0, a1)
        P1[rows, :] = jnp.where(lane < 64, low, jnp.where(lane < 96, ACCR[rows, :], 0.0))
        return carry

    lax.fori_loop(0, total // CHUNK, pack, 0)

    def p1_copy(h, d):
        i = h * 8 + d
        return remote(P1.at[rows_of(h, d)], PIN.at[rows_of(h, d)], p1_s.at[i], p1_r.at[i], partner(h, d))

    for h, d in groups:
        p1_copy(h, d).start()
    ring_step(UP, yu_s, yu_r, 1)
    for h, d in groups:
        p1_copy(h, d).wait_recv()

    def t_copy(h, d):
        i = h * 8 + d
        return remote(TS.at[pl.ds(h * half, half)], TIN.at[rows_of(h, d)], t_s.at[i], t_r.at[i], partner(h, d))

    lane_h = lax.broadcasted_iota(jnp.int32, (half, 128), 1)
    for h in range(2):
        s = P1[rows_of(h, 0), :]
        for d in range(1, 8):
            s = s + PIN[rows_of(h, d), :]
        rounded = s.astype(jnp.bfloat16).astype(jnp.float32)
        t0 = jnp.where(lane_h < 32, rounded, 0.0)
        t1 = jnp.where(jnp.logical_and(lane_h >= 32, lane_h < 64), rounded, 0.0)
        t0 = t0 + pltpu.roll(t0, 32, 1)
        t0 = t0 + pltpu.roll(t0, 64, 1)
        t1 = t1 + pltpu.roll(t1, 32, 1)
        t1 = t1 + pltpu.roll(t1, 64, 1)
        gap = jnp.sum(jnp.where(lane_h >= 64, s, 0.0), axis=1, keepdims=True)
        g0 = jax.nn.sigmoid(gap)
        pair = jnp.concatenate([g0 * t0, (1.0 - g0) * t1], axis=1).astype(jnp.bfloat16)
        TS[pl.ds(h * half, half), :] = pair
        TIN[rows_of(h, 0), :] = pair
        for hh, d in groups:
            if hh == h:
                t_copy(h, d).start()

    ring_step(UP, yu_s, yu_r, 2)
    for h, d in groups:
        t_copy(h, d).wait_recv()

    def spread(i, carry):
        rows = pl.ds(mult(i * CHUNK, CHUNK), CHUNK)
        c = CODE[rows, :]
        id0, id1 = c >> 5, c & 31
        t0 = TIN[rows, 0:128].astype(jnp.float32)
        t1 = TIN[rows, 128:256].astype(jnp.float32)
        for py in range(NY):
            named = group8 + py
            part = jnp.where(id0 == named, t0, jnp.where(id1 == named, t1, 0.0))
            A[rows, py * block : (py + 1) * block] = part.astype(jnp.bfloat16)
        return carry

    lax.fori_loop(0, total // CHUNK, spread, 0)
    ring_step(UP, yu_s, yu_r, 3)
    for b in range(per_class):
        into = FZ.at[pl.ds(b * fz_rows, fz_rows)]
        pltpu.make_async_copy(frozen, into, fz_r.at[b]).wait()
    ring_step(UP, yu_s, yu_r, 4)

    def rb_copy(h, d):
        i = h * 8 + d
        dst = res.at[pl.ds(h * half, half), own_cols]
        return remote(RB.at[rows_of(h, d)], dst, rb_s.at[i], rb_r.at[i], partner(h, d))

    def rb_local(h):
        dst = res.at[pl.ds(h * half, half), own_cols]
        return pltpu.make_async_copy(RB.at[rows_of(h, 0)], dst, rb_r.at[h * 8])

    def p2_copy(h, d):
        i = h * 8 + d
        return remote(PB.at[rows_of(h, d)], PIN2.at[rows_of(h, d)], p2_s.at[i], p2_r.at[i], partner(h, d))

    features = proj.shape[1]
    for i in (1, 3, 0, 2):
        rows = pl.ds(i * CHUNK, CHUNK)
        delta = jnp.dot(A[rows, :], UP[...], preferred_element_type=jnp.float32)
        combined = X[rows, :].astype(jnp.float32) + delta
        RB[rows, :] = combined.astype(jnp.bfloat16)
        blocks = range(i * (CHUNK // 64), (i + 1) * (CHUNK // 64))
        for k in reversed(blocks):
            if k % 8:
                rb_copy(k // 8, k % 8).start()
            else:
                rb_local(k // 8).start()
        square = combined * combined
        lanes = square[:, 0:128]
        for j in range(1, width // 128):
            lanes = lanes + square[:, j * 128 : (j + 1) * 128]
        scaled = (combined * gain[:, own_cols]).astype(jnp.bfloat16)
        part = jnp.dot(scaled, FZ[...], preferred_element_type=jnp.float32)
        PB[rows, 0:features] = part.astype(jnp.bfloat16)
        PB[rows, features : features + 128] = lanes.astype(jnp.bfloat16)
        for k in reversed(blocks):
            if k % 8:
                p2_copy(k // 8, k % 8).start()

    for h in range(2):
        for hh, d in groups:
            if hh == h:
                p2_copy(h, d).wait_recv()
        s = PB[rows_of(h, 0), :].astype(jnp.float32)
        for d in range(1, 8):
            s = s + PIN2[rows_of(h, d), :].astype(jnp.float32)
        mean = jnp.sum(s[:, features:], axis=1, keepdims=True) / tok.shape[1]
        proj[pl.ds(h * half, half), :] = (s[:, :features] * lax.rsqrt(mean + 1e-05)).astype(jnp.bfloat16)

    for h in range(2):
        rb_local(h).wait()
    for h, d in groups:
        rb_copy(h, d).wait_recv()
        for copy in (tok_copy, code_copy, p1_copy, t_copy, rb_copy, p2_copy):
            copy(h, d).wait_send()
    for d in range(1, 4):
        x_copy(down, DN, xd_s, xd_r, d).wait_send()
        x_copy(up, UP, xu_s, xu_r, d).wait_send()
    for c in range(4):
        for s in range(1, CHAINS[c][2] + 1):
            y_copy(DN, yd_s, yd_r, c, s).wait_send()
            y_copy(UP, yu_s, yu_r, c, s).wait_send()
    for k in range(NZ // 2):
        @pl.when(fz_other(k))
        def _():
            fz_copy(k).wait_send()


def shards(tokens, route_ids, router_weight, adapter_down, adapter_up, norm_gain, frozen_weight):
    rows, width = tokens.shape
    part = width // 8
    features = frozen_weight.shape[1]
    total = 8 * rows
    code = jnp.broadcast_to((route_ids[:, 0] * 32 + route_ids[:, 1])[:, None], (rows, 128))
    bf, f32 = jnp.bfloat16, jnp.float32
    dma = pltpu.SemaphoreType.DMA
    any_spec = pl.BlockSpec(memory_space=pl.ANY)
    vmem = pl.BlockSpec(memory_space=pltpu.VMEM)
    sems = [16] * 4 + [4] * 4 + [16] * 4 + [4] * 2 + [16] * 8 + [1]
    return pl.pallas_call(
        kernel,
        out_shape=(
            jax.ShapeDtypeStruct((rows, width), bf),
            jax.ShapeDtypeStruct((rows, features), bf),
        ),
        in_specs=[any_spec] * 6 + [vmem],
        out_specs=(any_spec, vmem),
        scratch_shapes=[
            pltpu.VMEM((total, part), bf),
            pltpu.VMEM((total, 128), jnp.int32),
            pltpu.VMEM((1024, part), bf),
            pltpu.VMEM((1024, part), bf),
            pltpu.VMEM((128, part), bf),
            pltpu.VMEM((part, features), bf),
            pltpu.VMEM((total, 128), f32),
            pltpu.VMEM((total, 128), f32),
            pltpu.VMEM((total, 128), f32),
            pltpu.VMEM((total, 128), f32),
            pltpu.VMEM((total, 128), f32),
            pltpu.VMEM((rows, 256), bf),
            pltpu.VMEM((total, 256), bf),
            pltpu.VMEM((total, 1024), bf),
            pltpu.VMEM((total, part), bf),
            pltpu.VMEM((total, features + 128), bf),
            pltpu.VMEM((total, features + 128), bf),
        ]
        + [dma((n,)) for n in sems],
        compiler_params=pltpu.CompilerParams(
            collective_id=0, has_side_effects=True, vmem_limit_bytes=48 * 1024 * 1024
        ),
        cost_estimate=pl.CostEstimate(flops=6_000_000_000, bytes_accessed=20_000_000, transcendentals=0),
    )(
        tokens,
        code,
        jnp.swapaxes(adapter_down[0], 0, 1),
        adapter_up[0],
        jnp.swapaxes(router_weight, 0, 1),
        frozen_weight,
        norm_gain[None, :],
    )


def solution(mesh):
    return jax.shard_map(
        shards,
        mesh=mesh,
        in_specs=(
            P(("fsdp", "adapter"), None),
            P(("fsdp", "adapter"), None),
            P(),
            P("adapter", None, None),
            P("adapter", None, None),
            P(),
            P("fsdp", None),
        ),
        out_specs=(P(("fsdp", "adapter"), None), P(("fsdp", "adapter"), None)),
        check_vma=False,
    )
```

```python
import functools

import jax
import jax.numpy as jnp
from jax import lax
from jax.experimental import pallas as pl
from jax.experimental.pallas import tpu as pltpu
from jax.sharding import PartitionSpec as P

MESH = pl.DeviceIdType.MESH
NX, NY, NZ = 8, 8, 8
CHUNK = 256


def mult(value, of):
    return pl.multiple_of(value, of)


def flip(bit, by):
    return bit + by * (1 - 2 * bit)


def kernel(
    tok, ids, down, up, router, frozen, gain, res, proj,
    X, IDS, CODE, DN, UP, RT, FZ, ACC0, ACC1, ACCR, P1, PIN, TS, TIN, A, RB, PB, PS, PO, PIN2,
    tok_s, tok_r, id_s, id_r, xd_s, xd_r, xu_s, xu_r, yd_s, yd_r, yu_s, yu_r,
    fz_s, fz_r, p1_s, p1_r, t_s, t_r, rb_s, rb_r, ps_s, ps_r, p2_s, p2_r, rt_sem,
):
    half = tok.shape[0] // 2
    width = X.shape[1]
    total = X.shape[0]
    rank = down.shape[0]
    block = 4 * rank
    features = proj.shape[1]
    per_class = width // frozen.shape[0]
    fs, ad = lax.axis_index("fsdp"), lax.axis_index("adapter")
    x_lo = lax.div(fs, 2 * NZ)
    z = lax.rem(lax.div(fs, 2), NZ)
    core = lax.rem(fs, 2)
    x_hi = lax.div(ad, NY)
    y = lax.rem(ad, NY)
    x = 2 * x_hi + x_lo
    zb = lax.rem(z, 2)
    mine = x_lo * 4 + zb * 2 + core

    def dev(px, py, pz, pc):
        return (lax.rem(px, 2) * (2 * NZ) + pz * 2 + pc, lax.div(px, 2) * NY + py)

    def partner(h, d):
        px, pz, pc = x, z, core
        if d & 4:
            px = x + 1 - 2 * x_lo if h == 0 else lax.rem(x + NX - 1 + 2 * x_lo, NX)
        if d & 2:
            pz = z + 1 - 2 * zb if h == 0 else lax.rem(z + NZ - 1 + 2 * zb, NZ)
        if d & 1:
            pc = 1 - core
        return dev(px, y, pz, pc)

    def member(d):
        return flip(x_lo, (d >> 2) & 1) * 4 + flip(zb, (d >> 1) & 1) * 2 + flip(core, d & 1)

    def cols_of(m):
        return pl.ds(mult(m * width, 128), width)

    own_cols = cols_of(mine)
    x_groups = [(h, d) for d in (6, 4, 7, 5) for h in range(2)]
    z_groups = [(h, d) for d in (2, 3, 1) for h in range(2)]
    groups = x_groups + z_groups

    def remote(src, dst, send, recv, device):
        return pltpu.make_async_remote_copy(
            src_ref=src, dst_ref=dst, send_sem=send, recv_sem=recv, device_id=device, device_id_type=MESH
        )

    def rows_of(h, d):
        return pl.ds((h * 8 + d) * half, half)

    def tok_copy(h, d):
        i = h * 8 + d
        src = tok.at[pl.ds(h * half, half), cols_of(member(d))]
        return remote(src, X.at[rows_of(h, d)], tok_s.at[i], tok_r.at[i], partner(h, d))

    def id_copy(h, d):
        i = h * 8 + d
        return remote(ids, IDS.at[i], id_s.at[i], id_r.at[i], partner(h, d))

    def tok_local(h):
        cp = pltpu.make_async_copy(tok.at[pl.ds(h * half, half), own_cols], X.at[rows_of(h, 0)], tok_r.at[h * 8])
        cq = pltpu.make_async_copy(ids, IDS.at[h * 8], id_r.at[h * 8])
        return cp, cq

    def slot(py, px_hi):
        return pl.ds(mult(py * block + px_hi * rank, rank), rank)

    def x_copy(src, buf, send, recv, i):
        px = lax.rem(x + (2 * x_lo - 1) * i + NX, NX)
        cols = cols_of(lax.rem(px, 2) * 4 + zb * 2 + core)
        return remote(src.at[:, cols], buf.at[slot(y, x_hi)], send.at[i], recv.at[i], dev(px, y, z, core))

    def x_source(i):
        return lax.rem(x + (1 - 2 * x_lo) * (-i if i % 2 else i) + NX, NX)

    def x_local(src, buf, recv):
        return pltpu.make_async_copy(src.at[:, own_cols], buf.at[slot(y, x_hi)], recv.at[0])

    def steps(q, way):
        return 4 if (q < 2) == (way == 1) else 3

    def y_copy(buf, send, recv, q, way, s):
        origin = lax.rem(y + NY - way * (s - 1), NY)
        rows = slot(origin, lax.div(x_source(q), 2) if q else x_hi)
        device = dev(x, lax.rem(y + NY + way, NY), z, core)
        i = (q * 2 + (way + 1) // 2) * 4 + s - 1
        return remote(buf.at[rows], buf.at[rows], send.at[i], recv.at[i], device)

    def ring_start(buf, send, recv, q):
        for way in (1, -1):
            y_copy(buf, send, recv, q, way, 1).start()

    def ring_step(buf, send, recv, s):
        for q in range(4):
            for way in (1, -1):
                if s <= steps(q, way):
                    y_copy(buf, send, recv, q, way, s).wait_recv()
                    if s < steps(q, way):
                        y_copy(buf, send, recv, q, way, s + 1).start()

    fz_class = lax.div(fs, per_class)
    fz_core = lax.rem(fz_class, 2)
    fz_zb = lax.rem(lax.div(fz_class, 2), 2)
    fz_rows = frozen.shape[0]
    fz_slot = pl.ds(mult(lax.rem(fs, per_class) * fz_rows, 16), fz_rows)
    fz_self = fz_class == mine

    def fz_other(k):
        return jnp.logical_not(jnp.logical_and(2 * k + fz_zb == z, fz_core == core))

    def fz_copy(k):
        device = dev(x, y, 2 * k + fz_zb, fz_core)
        return remote(frozen, FZ.at[fz_slot], fz_s.at[k], fz_r.at[lax.rem(fs, per_class)], device)

    barrier = pltpu.get_barrier_semaphore()

    def greet(device):
        pl.semaphore_signal(barrier, inc=1, device_id=device, device_id_type=MESH)

    for i in range(1, 4):
        greet(dev(x_source(i), y, z, core))
    for way in (1, -1):
        greet(dev(x, lax.rem(y + NY + way, NY), z, core))
    for h, d in groups:
        greet(partner(h, d))
    for b in range(per_class):
        source = mine * per_class + b

        @pl.when(source != fs)
        def _():
            greet((source, ad))

    x_local(down, DN, xd_r).start()
    x_local(up, UP, xu_r).start()
    RT[...] = jnp.zeros_like(RT)
    rt_copy = pltpu.make_async_copy(router.at[:, own_cols], RT.at[pl.ds(2 * rank, rank)], rt_sem.at[0])
    rt_copy.start()
    for h in range(2):
        for c in tok_local(h):
            c.start()
    pl.semaphore_wait(barrier, 14 + 3 + 2 + NZ // 2 - fz_self.astype(jnp.int32))

    for i in range(1, 4):
        x_copy(down, DN, xd_s, xd_r, i).start()
    x_local(down, DN, xd_r).wait()
    ring_start(DN, yd_s, yd_r, 0)
    for h, d in groups:
        id_copy(h, d).start()
    for h, d in z_groups:
        tok_copy(h, d).start()

    for i in range(1, 4):
        x_copy(down, DN, xd_s, xd_r, i).wait_recv()
        ring_start(DN, yd_s, yd_r, i)
    for h, d in x_groups:
        tok_copy(h, d).start()
    for i in range(1, 4):
        x_copy(up, UP, xu_s, xu_r, i).start()

    ring_step(DN, yd_s, yd_r, 1)
    ring_step(DN, yd_s, yd_r, 2)

    for h in range(2):
        for c in tok_local(h):
            c.wait()
    for h, d in groups:
        id_copy(h, d).wait_recv()
    for h in range(2):
        for d in range(8):
            pair = IDS[h * 8 + d]
            both = (pair[0:1, :] * 32 + pair[1:2, :]).astype(jnp.float32)
            spread_out = jnp.transpose(jnp.broadcast_to(both, (128, 128)))
            CODE[rows_of(h, d), :] = spread_out[h * half : (h + 1) * half, :].astype(jnp.int32)
    for h, d in z_groups + x_groups:
        tok_copy(h, d).wait_recv()
    rt_copy.wait()
    for k in range(NZ // 2):
        @pl.when(fz_other(k))
        def _():
            fz_copy(k).start()

    @pl.when(fz_self)
    def _():
        pltpu.make_async_copy(frozen, FZ.at[fz_slot], fz_r.at[lax.rem(fs, per_class)]).start()

    lane = lax.broadcasted_iota(jnp.int32, (CHUNK, 128), 1)
    group8 = (lane >> 5) * 8
    nt = (((1,), (1,)), ((), ()))

    def low_rank(py, first=False):
        def body(i, carry):
            rows = pl.ds(mult(i * CHUNK, CHUNK), CHUNK)
            xs = X[rows, :]
            got = lax.dot_general(
                xs, DN[pl.ds(mult(py * block, block), block), :], nt, preferred_element_type=jnp.float32
            )
            c = CODE[rows, :]
            id0, id1 = c >> 5, c & 31
            named = group8 + py
            part0 = jnp.where(id0 == named, got, 0.0)
            part1 = jnp.where(id1 == named, got, 0.0)
            if first:
                ACC0[rows, :] = part0
                ACC1[rows, :] = part1
                logit = lax.dot_general(xs, RT[...], nt, preferred_element_type=jnp.float32)
                at = lane - 64
                ACCR[rows, :] = jnp.where(at == id0, logit, 0.0) - jnp.where(at == id1, logit, 0.0)
            else:
                ACC0[rows, :] += part0
                ACC1[rows, :] += part1
            return carry

        lax.fori_loop(0, total // CHUNK, body, 0)

    low_rank(y, True)
    ring_step(DN, yd_s, yd_r, 3)
    x_local(up, UP, xu_r).wait()
    ring_start(UP, yu_s, yu_r, 0)
    for i in range(1, 4):
        x_copy(up, UP, xu_s, xu_r, i).wait_recv()
        ring_start(UP, yu_s, yu_r, i)
    for s in (1, 2):
        low_rank(lax.rem(y + NY - s, NY))
        low_rank(lax.rem(y + s, NY))
    ring_step(DN, yd_s, yd_r, 4)
    low_rank(lax.rem(y + NY - 3, NY))
    low_rank(lax.rem(y + 3, NY))
    low_rank(lax.rem(y + 4, NY))

    def pack(i, carry):
        rows = pl.ds(mult(i * CHUNK, CHUNK), CHUNK)
        a0, a1 = ACC0[rows, :], ACC1[rows, :]
        a0 = a0 + pltpu.roll(a0, 64, 1)
        a0 = a0 + pltpu.roll(a0, 32, 1)
        a1 = a1 + pltpu.roll(a1, 64, 1)
        a1 = a1 + pltpu.roll(a1, 32, 1)
        low = jnp.where(lane < 32, a0, a1)
        P1[rows, :] = jnp.where(lane < 64, low, jnp.where(lane < 96, ACCR[rows, :], 0.0))
        return carry

    lax.fori_loop(0, total // CHUNK, pack, 0)

    def p1_copy(h, d):
        i = h * 8 + d
        return remote(P1.at[rows_of(h, d)], PIN.at[rows_of(h, d)], p1_s.at[i], p1_r.at[i], partner(h, d))

    for h, d in groups:
        p1_copy(h, d).start()
    ring_step(UP, yu_s, yu_r, 1)
    for h, d in groups:
        p1_copy(h, d).wait_recv()

    def t_copy(h, d):
        i = h * 8 + d
        return remote(TS.at[pl.ds(h * half, half)], TIN.at[rows_of(h, d)], t_s.at[i], t_r.at[i], partner(h, d))

    lane_h = lax.broadcasted_iota(jnp.int32, (half, 128), 1)
    for h in range(2):
        s = P1[rows_of(h, 0), :]
        for d in range(1, 8):
            s = s + PIN[rows_of(h, d), :]
        rounded = s.astype(jnp.bfloat16).astype(jnp.float32)
        gap = jnp.sum(jnp.where(lane_h >= 64, s, 0.0), axis=1, keepdims=True)
        g0 = jax.nn.sigmoid(gap)
        gated = rounded * jnp.where(lane_h < 32, g0, 1.0 - g0)
        pair = jnp.where(lane_h < 64, gated, 0.0).astype(jnp.bfloat16)
        TS[pl.ds(h * half, half), :] = pair
        TIN[rows_of(h, 0), :] = pair
        for hh, d in groups:
            if hh == h:
                t_copy(h, d).start()

    ring_step(UP, yu_s, yu_r, 2)
    for h, d in groups:
        t_copy(h, d).wait_recv()

    def spread(i, carry):
        rows = pl.ds(mult(i * CHUNK, CHUNK), CHUNK)
        c = CODE[rows, :]
        id0, id1 = c >> 5, c & 31
        t = TIN[rows, :].astype(jnp.float32)
        t0 = jnp.where(lane < 32, t, 0.0)
        t1 = t - t0
        t0 = t0 + pltpu.roll(t0, 32, 1)
        t0 = t0 + pltpu.roll(t0, 64, 1)
        t1 = t1 + pltpu.roll(t1, 32, 1)
        t1 = t1 + pltpu.roll(t1, 64, 1)
        for py in range(NY):
            named = group8 + py
            part = jnp.where(id0 == named, t0, jnp.where(id1 == named, t1, 0.0))
            A[rows, py * block : (py + 1) * block] = part.astype(jnp.bfloat16)
        return carry

    lax.fori_loop(0, total // CHUNK, spread, 0)
    ring_step(UP, yu_s, yu_r, 3)
    for b in range(per_class):
        into = FZ.at[pl.ds(b * fz_rows, fz_rows)]
        pltpu.make_async_copy(frozen, into, fz_r.at[b]).wait()
    ring_step(UP, yu_s, yu_r, 4)

    def rb_copy(h, d):
        i = h * 8 + d
        dst = res.at[pl.ds(h * half, half), own_cols]
        return remote(RB.at[rows_of(h, d)], dst, rb_s.at[i], rb_r.at[i], partner(h, d))

    def rb_local(h):
        dst = res.at[pl.ds(h * half, half), own_cols]
        return pltpu.make_async_copy(RB.at[rows_of(h, 0)], dst, rb_r.at[h * 8])

    def ps_copy(h, d):
        i = h * 8 + d
        return remote(PB.at[rows_of(h, d)], PS.at[rows_of(h, d - 1)], ps_s.at[i], ps_r.at[i], partner(0, 1))

    def p2_copy(h, d):
        i = h * 8 + d
        return remote(PO.at[rows_of(h, d)], PIN2.at[rows_of(h, d)], p2_s.at[i], p2_r.at[i], partner(h, d))

    for i in (1, 3, 0, 2):
        rows = pl.ds(i * CHUNK, CHUNK)
        delta = jnp.dot(A[rows, :], UP[...], preferred_element_type=jnp.float32)
        combined = X[rows, :].astype(jnp.float32) + delta
        RB[rows, :] = combined.astype(jnp.bfloat16)
        blocks = [(4 * i + k) for k in (2, 0, 3, 1)]
        for k in blocks:
            if k % 8:
                rb_copy(k // 8, k % 8).start()
            else:
                rb_local(k // 8).start()
        square = combined * combined
        lanes = square[:, 0:128]
        for j in range(1, width // 128):
            lanes = lanes + square[:, j * 128 : (j + 1) * 128]
        scaled = (combined * gain[:, own_cols]).astype(jnp.bfloat16)
        PB[rows, 0:features] = jnp.dot(scaled, FZ[...], preferred_element_type=jnp.float32)
        PB[rows, features : features + 128] = lanes
        for k in blocks:
            if k % 2:
                ps_copy(k // 8, k % 8).start()

    for d in (6, 4, 2):
        for h in range(2):
            ps_copy(h, d + 1).wait_recv()
            rows = rows_of(h, d)
            PO[rows, :] = (PB[rows, :] + PS[rows, :]).astype(jnp.bfloat16)
            p2_copy(h, d).start()

    for h in range(2):
        ps_copy(h, 1).wait_recv()
        s = PB[rows_of(h, 0), :] + PS[rows_of(h, 0), :]
        for d in (6, 4, 2):
            p2_copy(h, d).wait_recv()
            s = s + PIN2[rows_of(h, d), :].astype(jnp.float32)
        mean = jnp.sum(s[:, features:], axis=1, keepdims=True) / tok.shape[1]
        proj[pl.ds(h * half, half), :] = (s[:, :features] * lax.rsqrt(mean + 1e-05)).astype(jnp.bfloat16)

    for h in range(2):
        rb_local(h).wait()
    for h, d in groups:
        rb_copy(h, d).wait_recv()
        for copy in (tok_copy, id_copy, p1_copy, t_copy, rb_copy):
            copy(h, d).wait_send()
    for h in range(2):
        for d in (1, 3, 5, 7):
            ps_copy(h, d).wait_send()
        for d in (2, 4, 6):
            p2_copy(h, d).wait_send()
    for i in range(1, 4):
        x_copy(down, DN, xd_s, xd_r, i).wait_send()
        x_copy(up, UP, xu_s, xu_r, i).wait_send()
    for q in range(4):
        for way in (1, -1):
            for s in range(1, steps(q, way) + 1):
                y_copy(DN, yd_s, yd_r, q, way, s).wait_send()
                y_copy(UP, yu_s, yu_r, q, way, s).wait_send()
    for k in range(NZ // 2):
        @pl.when(fz_other(k))
        def _():
            fz_copy(k).wait_send()


def shards(tokens, route_ids, router_weight, adapter_down, adapter_up, norm_gain, frozen_weight):
    rows, width = tokens.shape
    part = width // 8
    features = frozen_weight.shape[1]
    total = 8 * rows
    bf, f32 = jnp.bfloat16, jnp.float32
    dma = pltpu.SemaphoreType.DMA
    any_spec = pl.BlockSpec(memory_space=pltpu.HBM)
    vmem = pl.BlockSpec(memory_space=pltpu.VMEM)
    sems = [16] * 4 + [4] * 4 + [32] * 4 + [4] * 2 + [16] * 10 + [1]
    return pl.pallas_call(
        kernel,
        out_shape=(
            jax.ShapeDtypeStruct((rows, width), bf),
            jax.ShapeDtypeStruct((rows, features), bf),
        ),
        in_specs=[any_spec] * 6 + [vmem],
        out_specs=(any_spec, vmem),
        scratch_shapes=[
            pltpu.VMEM((total, part), bf),
            pltpu.VMEM((16, 2, rows), jnp.int32),
            pltpu.VMEM((total, 128), jnp.int32),
            pltpu.VMEM((1024, part), bf),
            pltpu.VMEM((1024, part), bf),
            pltpu.VMEM((128, part), bf),
            pltpu.VMEM((part, features), bf),
            pltpu.VMEM((total, 128), f32),
            pltpu.VMEM((total, 128), f32),
            pltpu.VMEM((total, 128), f32),
            pltpu.VMEM((total, 128), f32),
            pltpu.VMEM((total, 128), f32),
            pltpu.VMEM((rows, 128), bf),
            pltpu.VMEM((total, 128), bf),
            pltpu.VMEM((total, 1024), bf),
            pltpu.VMEM((total, part), bf),
            pltpu.VMEM((total, features + 128), f32),
            pltpu.VMEM((total, features + 128), f32),
            pltpu.VMEM((total, features + 128), bf),
            pltpu.VMEM((total, features + 128), bf),
        ]
        + [dma((n,)) for n in sems],
        compiler_params=pltpu.CompilerParams(
            collective_id=0, has_side_effects=True, vmem_limit_bytes=60 * 1024 * 1024
        ),
        cost_estimate=pl.CostEstimate(flops=6_000_000_000, bytes_accessed=20_000_000, transcendentals=0),
    )(
        tokens,
        jnp.swapaxes(route_ids, 0, 1),
        jnp.swapaxes(adapter_down[0], 0, 1),
        adapter_up[0],
        jnp.swapaxes(router_weight, 0, 1),
        frozen_weight,
        norm_gain[None, :],
    )


def solution(mesh):
    return jax.shard_map(
        shards,
        mesh=mesh,
        in_specs=(
            P(("fsdp", "adapter"), None),
            P(("fsdp", "adapter"), None),
            P(),
            P("adapter", None, None),
            P("adapter", None, None),
            P(),
            P("fsdp", None),
        ),
        out_specs=(P(("fsdp", "adapter"), None), P(("fsdp", "adapter"), None)),
        check_vma=False,
    )
```

```python
import functools

import jax
import jax.numpy as jnp
from jax import lax
from jax.experimental import pallas as pl
from jax.experimental.pallas import tpu as pltpu
from jax.sharding import PartitionSpec as P

MESH = pl.DeviceIdType.MESH
NX, NY, NZ = 8, 8, 8
CHUNK = 256


def mult(value, of):
    return pl.multiple_of(value, of)


def flip(bit, by):
    return bit + by * (1 - 2 * bit)


def kernel(
    tok, ids, down, up, router, frozen, gain, res, proj,
    X, IDS, CODE, DN, UP, RT, FZ, ACC0, ACC1, ACCR, P1, PIN, TS, TIN, A, RB, PB, PS, PO, PIN2, GAIN,
    tok_s, tok_r, id_s, id_r, xd_s, xd_r, xu_s, xu_r, yd_s, yd_r, yu_s, yu_r,
    fz_s, fz_r, p1_s, p1_r, t_s, t_r, rb_s, rb_r, ps_s, ps_r, p2_s, p2_r, rt_sem,
):
    half = tok.shape[0] // 2
    width = X.shape[1]
    total = X.shape[0]
    rank = down.shape[0]
    block = 4 * rank
    features = proj.shape[1]
    per_class = width // frozen.shape[0]
    fs, ad = lax.axis_index("fsdp"), lax.axis_index("adapter")
    x_lo = lax.div(fs, 2 * NZ)
    z = lax.rem(lax.div(fs, 2), NZ)
    core = lax.rem(fs, 2)
    x_hi = lax.div(ad, NY)
    y = lax.rem(ad, NY)
    x = 2 * x_hi + x_lo
    zb = lax.rem(z, 2)
    mine = x_lo * 4 + zb * 2 + core

    def dev(px, py, pz, pc):
        return (lax.rem(px, 2) * (2 * NZ) + pz * 2 + pc, lax.div(px, 2) * NY + py)

    def partner(h, d):
        px, pz, pc = x, z, core
        if d & 4:
            px = x + 1 - 2 * x_lo if h == 0 else lax.rem(x + NX - 1 + 2 * x_lo, NX)
        if d & 2:
            pz = z + 1 - 2 * zb if h == 0 else lax.rem(z + NZ - 1 + 2 * zb, NZ)
        if d & 1:
            pc = 1 - core
        return dev(px, y, pz, pc)

    def member(d):
        return flip(x_lo, (d >> 2) & 1) * 4 + flip(zb, (d >> 1) & 1) * 2 + flip(core, d & 1)

    def cols_of(m):
        return pl.ds(mult(m * width, 128), width)

    own_cols = cols_of(mine)
    x_groups = [(h, d) for d in (6, 4, 7, 5) for h in range(2)]
    z_groups = [(h, d) for d in (2, 3, 1) for h in range(2)]
    groups = x_groups + z_groups

    def remote(src, dst, send, recv, device):
        return pltpu.make_async_remote_copy(
            src_ref=src, dst_ref=dst, send_sem=send, recv_sem=recv, device_id=device, device_id_type=MESH
        )

    def rows_of(h, d):
        return pl.ds((h * 8 + d) * half, half)

    def tok_copy(h, d):
        i = h * 8 + d
        src = tok.at[pl.ds(h * half, half), cols_of(member(d))]
        return remote(src, X.at[rows_of(h, d)], tok_s.at[i], tok_r.at[i], partner(h, d))

    def id_copy(h, d):
        i = h * 8 + d
        return remote(ids, IDS.at[i], id_s.at[i], id_r.at[i], partner(h, d))

    def tok_local(h):
        cp = pltpu.make_async_copy(tok.at[pl.ds(h * half, half), own_cols], X.at[rows_of(h, 0)], tok_r.at[h * 8])
        cq = pltpu.make_async_copy(ids, IDS.at[h * 8], id_r.at[h * 8])
        return cp, cq

    def slot(py, px_hi):
        return pl.ds(mult(py * block + px_hi * rank, rank), rank)

    def x_copy(src, buf, send, recv, i):
        px = lax.rem(x + (2 * x_lo - 1) * i + NX, NX)
        cols = cols_of(lax.rem(px, 2) * 4 + zb * 2 + core)
        return remote(src.at[:, cols], buf.at[slot(y, x_hi)], send.at[i], recv.at[i], dev(px, y, z, core))

    def x_source(i):
        return lax.rem(x + (1 - 2 * x_lo) * (-i if i % 2 else i) + NX, NX)

    def x_local(src, buf, recv):
        return pltpu.make_async_copy(src.at[:, own_cols], buf.at[slot(y, x_hi)], recv.at[0])

    def steps(q, way):
        return 4 if (q < 2) == (way == 1) else 3

    def y_copy(buf, send, recv, q, way, s):
        origin = lax.rem(y + NY - way * (s - 1), NY)
        rows = slot(origin, lax.div(x_source(q), 2) if q else x_hi)
        device = dev(x, lax.rem(y + NY + way, NY), z, core)
        i = (q * 2 + (way + 1) // 2) * 4 + s - 1
        return remote(buf.at[rows], buf.at[rows], send.at[i], recv.at[i], device)

    def ring_start(buf, send, recv, q):
        for way in (1, -1):
            y_copy(buf, send, recv, q, way, 1).start()

    def ring_step(buf, send, recv, s):
        for q in range(4):
            for way in (1, -1):
                if s <= steps(q, way):
                    y_copy(buf, send, recv, q, way, s).wait_recv()
                    if s < steps(q, way):
                        y_copy(buf, send, recv, q, way, s + 1).start()

    fz_class = lax.div(fs, per_class)
    fz_core = lax.rem(fz_class, 2)
    fz_zb = lax.rem(lax.div(fz_class, 2), 2)
    fz_rows = frozen.shape[0]
    fz_slot = pl.ds(mult(lax.rem(fs, per_class) * fz_rows, 16), fz_rows)
    fz_self = fz_class == mine

    def fz_other(k):
        return jnp.logical_not(jnp.logical_and(2 * k + fz_zb == z, fz_core == core))

    def fz_copy(k):
        device = dev(x, y, 2 * k + fz_zb, fz_core)
        return remote(frozen, FZ.at[fz_slot], fz_s.at[k], fz_r.at[lax.rem(fs, per_class)], device)

    barrier = pltpu.get_barrier_semaphore()

    def greet(device):
        pl.semaphore_signal(barrier, inc=1, device_id=device, device_id_type=MESH)

    for i in range(1, 4):
        greet(dev(x_source(i), y, z, core))
    for way in (1, -1):
        greet(dev(x, lax.rem(y + NY + way, NY), z, core))
    for h, d in groups:
        greet(partner(h, d))
    for b in range(per_class):
        source = mine * per_class + b

        @pl.when(source != fs)
        def _():
            greet((source, ad))

    x_local(down, DN, xd_r).start()
    x_local(up, UP, xu_r).start()
    RT[...] = jnp.zeros_like(RT)
    rt_copy = pltpu.make_async_copy(router.at[:, own_cols], RT.at[pl.ds(2 * rank, rank)], rt_sem.at[0])
    rt_copy.start()
    gain_copy = pltpu.make_async_copy(gain.at[:, own_cols], GAIN, rt_sem.at[1])
    gain_copy.start()
    for h in range(2):
        for c in tok_local(h):
            c.start()
    pl.semaphore_wait(barrier, 14 + 3 + 2 + NZ // 2 - fz_self.astype(jnp.int32))

    for i in range(1, 4):
        x_copy(down, DN, xd_s, xd_r, i).start()
    x_local(down, DN, xd_r).wait()
    ring_start(DN, yd_s, yd_r, 0)
    for h, d in groups:
        id_copy(h, d).start()
    for h, d in z_groups:
        tok_copy(h, d).start()

    for i in range(1, 4):
        x_copy(down, DN, xd_s, xd_r, i).wait_recv()
        ring_start(DN, yd_s, yd_r, i)
    for h, d in x_groups:
        tok_copy(h, d).start()

    lane = lax.broadcasted_iota(jnp.int32, (CHUNK, 128), 1)
    group8 = (lane >> 5) * 8
    nt = (((1,), (1,)), ((), ()))

    def take_ids():
        for h in range(2):
            tok_local(h)[1].wait()
        for h, d in groups:
            id_copy(h, d).wait_recv()
        for h in range(2):
            for d in range(8):
                pair = IDS[h * 8 + d]
                both = (pair[0:1, :] * 32 + pair[1:2, :]).astype(jnp.float32)
                down_rows = jnp.transpose(jnp.broadcast_to(both, (128, 128)))
                CODE[rows_of(h, d), :] = down_rows[h * half : (h + 1) * half, :].astype(jnp.int32)

    def take_tokens():
        for h in range(2):
            tok_local(h)[0].wait()
        for h, d in z_groups + x_groups:
            tok_copy(h, d).wait_recv()
        rt_copy.wait()
        gain_copy.wait()

    def send_frozen():
        for k in range(NZ // 2):
            @pl.when(fz_other(k))
            def _():
                fz_copy(k).start()

        @pl.when(fz_self)
        def _():
            pltpu.make_async_copy(frozen, FZ.at[fz_slot], fz_r.at[lax.rem(fs, per_class)]).start()

    def low_rank(py, first=False):
        def body(i, carry):
            rows = pl.ds(mult(i * CHUNK, CHUNK), CHUNK)
            xs = X[rows, :]
            got = lax.dot_general(
                xs, DN[pl.ds(mult(py * block, block), block), :], nt, preferred_element_type=jnp.float32
            )
            c = CODE[rows, :]
            id0, id1 = c >> 5, c & 31
            named = group8 + py
            part0 = jnp.where(id0 == named, got, 0.0)
            part1 = jnp.where(id1 == named, got, 0.0)
            if first:
                ACC0[rows, :] = part0
                ACC1[rows, :] = part1
                logit = lax.dot_general(xs, RT[...], nt, preferred_element_type=jnp.float32)
                at = lane - 64
                ACCR[rows, :] = jnp.where(at == id0, logit, 0.0) - jnp.where(at == id1, logit, 0.0)
            else:
                ACC0[rows, :] += part0
                ACC1[rows, :] += part1
            return carry

        lax.fori_loop(0, total // CHUNK, body, 0)

    def low_rank_at(s):
        low_rank(lax.rem(y + NY - s, NY))
        if s < 4:
            low_rank(lax.rem(y + s, NY))

    def p1_copy(h, d):
        i = h * 8 + d
        return remote(P1.at[rows_of(h, d)], PIN.at[rows_of(h, d)], p1_s.at[i], p1_r.at[i], partner(h, d))

    def send_partials():
        def pack(i, carry):
            rows = pl.ds(mult(i * CHUNK, CHUNK), CHUNK)
            a0, a1 = ACC0[rows, :], ACC1[rows, :]
            a0 = a0 + pltpu.roll(a0, 64, 1)
            a0 = a0 + pltpu.roll(a0, 32, 1)
            a1 = a1 + pltpu.roll(a1, 64, 1)
            a1 = a1 + pltpu.roll(a1, 32, 1)
            low = jnp.where(lane < 32, a0, a1)
            P1[rows, :] = jnp.where(lane < 64, low, jnp.where(lane < 96, ACCR[rows, :], 0.0))
            return carry

        lax.fori_loop(0, total // CHUNK, pack, 0)
        for h, d in groups:
            p1_copy(h, d).start()

    def t_copy(h, d):
        i = h * 8 + d
        return remote(TS.at[pl.ds(h * half, half)], TIN.at[rows_of(h, d)], t_s.at[i], t_r.at[i], partner(h, d))

    def send_gated():
        lane_h = lax.broadcasted_iota(jnp.int32, (half, 128), 1)
        for h in range(2):
            for hh, d in groups:
                if hh == h:
                    p1_copy(h, d).wait_recv()
            s = P1[rows_of(h, 0), :]
            for d in range(1, 8):
                s = s + PIN[rows_of(h, d), :]
            rounded = s.astype(jnp.bfloat16).astype(jnp.float32)
            gap = jnp.sum(jnp.where(lane_h >= 64, s, 0.0), axis=1, keepdims=True)
            g0 = jax.nn.sigmoid(gap)
            gated = rounded * jnp.where(lane_h < 32, g0, 1.0 - g0)
            pair = jnp.where(lane_h < 64, gated, 0.0).astype(jnp.bfloat16)
            TS[pl.ds(h * half, half), :] = pair
            TIN[rows_of(h, 0), :] = pair
            for hh, d in groups:
                if hh == h:
                    t_copy(h, d).start()

    def take_gated():
        for h, d in groups:
            t_copy(h, d).wait_recv()

        def spread(i, carry):
            rows = pl.ds(mult(i * CHUNK, CHUNK), CHUNK)
            c = CODE[rows, :]
            id0, id1 = c >> 5, c & 31
            t = TIN[rows, :].astype(jnp.float32)
            t0 = jnp.where(lane < 32, t, 0.0)
            t1 = t - t0
            t0 = t0 + pltpu.roll(t0, 32, 1)
            t0 = t0 + pltpu.roll(t0, 64, 1)
            t1 = t1 + pltpu.roll(t1, 32, 1)
            t1 = t1 + pltpu.roll(t1, 64, 1)
            for py in range(NY):
                named = group8 + py
                part = jnp.where(id0 == named, t0, jnp.where(id1 == named, t1, 0.0))
                A[rows, py * block : (py + 1) * block] = part.astype(jnp.bfloat16)
            return carry

        lax.fori_loop(0, total // CHUNK, spread, 0)

    def down_step(s):
        ring_step(DN, yd_s, yd_r, s)

    def up_step(s):
        ring_step(UP, yu_s, yu_r, s)

    def up_send():
        for i in range(1, 4):
            x_copy(up, UP, xu_s, xu_r, i).start()

    def up_start():
        x_local(up, UP, xu_r).wait()
        ring_start(UP, yu_s, yu_r, 0)
        for i in range(1, 4):
            x_copy(up, UP, xu_s, xu_r, i).wait_recv()
            ring_start(UP, yu_s, yu_r, i)

    send_frozen()
    up_send()
    take_ids()
    down_step(1)
    down_step(2)
    take_tokens()
    low_rank(y, True)
    low_rank_at(1)
    down_step(3)
    up_start()
    low_rank_at(2)
    low_rank_at(3)
    down_step(4)
    low_rank_at(4)
    send_partials()
    up_step(1)
    send_gated()
    up_step(2)
    take_gated()
    up_step(3)
    up_step(4)
    for b in range(per_class):
        into = FZ.at[pl.ds(b * fz_rows, fz_rows)]
        pltpu.make_async_copy(frozen, into, fz_r.at[b]).wait()

    def rb_copy(h, d):
        i = h * 8 + d
        dst = res.at[pl.ds(h * half, half), own_cols]
        return remote(RB.at[rows_of(h, d)], dst, rb_s.at[i], rb_r.at[i], partner(h, d))

    def rb_local(h):
        dst = res.at[pl.ds(h * half, half), own_cols]
        return pltpu.make_async_copy(RB.at[rows_of(h, 0)], dst, rb_r.at[h * 8])

    def ps_copy(h, d):
        i = h * 8 + d
        return remote(PB.at[rows_of(h, d)], PS.at[rows_of(h, d - 1)], ps_s.at[i], ps_r.at[i], partner(0, 1))

    def p2_copy(h, d):
        i = h * 8 + d
        return remote(PO.at[rows_of(h, d)], PIN2.at[rows_of(h, d)], p2_s.at[i], p2_r.at[i], partner(h, d))

    for i in (1, 3, 0, 2):
        rows = pl.ds(i * CHUNK, CHUNK)
        delta = jnp.dot(A[rows, :], UP[...], preferred_element_type=jnp.float32)
        combined = X[rows, :].astype(jnp.float32) + delta
        RB[rows, :] = combined.astype(jnp.bfloat16)
        blocks = [(4 * i + k) for k in (2, 0, 3, 1)]
        for k in blocks:
            if k % 8:
                rb_copy(k // 8, k % 8).start()
            else:
                rb_local(k // 8).start()
        square = combined * combined
        lanes = square[:, 0:128]
        for j in range(1, width // 128):
            lanes = lanes + square[:, j * 128 : (j + 1) * 128]
        scaled = (combined * GAIN[...]).astype(jnp.bfloat16)
        PB[rows, 0:features] = jnp.dot(scaled, FZ[...], preferred_element_type=jnp.float32)
        PB[rows, features : features + 128] = lanes
        for k in blocks:
            if k % 2:
                ps_copy(k // 8, k % 8).start()

    for d in (6, 4, 2):
        for h in range(2):
            ps_copy(h, d + 1).wait_recv()
            rows = rows_of(h, d)
            PO[rows, :] = (PB[rows, :] + PS[rows, :]).astype(jnp.bfloat16)
            p2_copy(h, d).start()

    for h in range(2):
        ps_copy(h, 1).wait_recv()
        s = PB[rows_of(h, 0), :] + PS[rows_of(h, 0), :]
        for d in (6, 4, 2):
            p2_copy(h, d).wait_recv()
            s = s + PIN2[rows_of(h, d), :].astype(jnp.float32)
        mean = jnp.sum(s[:, features:], axis=1, keepdims=True) / tok.shape[1]
        proj[pl.ds(h * half, half), :] = (s[:, :features] * lax.rsqrt(mean + 1e-05)).astype(jnp.bfloat16)

    for h in range(2):
        rb_local(h).wait()
    for h, d in groups:
        rb_copy(h, d).wait_recv()
        for copy in (tok_copy, id_copy, p1_copy, t_copy, rb_copy):
            copy(h, d).wait_send()
    for h in range(2):
        for d in (1, 3, 5, 7):
            ps_copy(h, d).wait_send()
        for d in (2, 4, 6):
            p2_copy(h, d).wait_send()
    for i in range(1, 4):
        x_copy(down, DN, xd_s, xd_r, i).wait_send()
        x_copy(up, UP, xu_s, xu_r, i).wait_send()
    for q in range(4):
        for way in (1, -1):
            for s in range(1, steps(q, way) + 1):
                y_copy(DN, yd_s, yd_r, q, way, s).wait_send()
                y_copy(UP, yu_s, yu_r, q, way, s).wait_send()
    for k in range(NZ // 2):
        @pl.when(fz_other(k))
        def _():
            fz_copy(k).wait_send()


def shards(tokens, route_ids, router_weight, adapter_down, adapter_up, norm_gain, frozen_weight):
    rows, width = tokens.shape
    part = width // 8
    features = frozen_weight.shape[1]
    total = 8 * rows
    bf, f32 = jnp.bfloat16, jnp.float32
    dma = pltpu.SemaphoreType.DMA
    any_spec = pl.BlockSpec(memory_space=pltpu.HBM)
    vmem = pl.BlockSpec(memory_space=pltpu.VMEM)
    sems = [16] * 4 + [4] * 4 + [32] * 4 + [4] * 2 + [16] * 10 + [2]
    return pl.pallas_call(
        kernel,
        out_shape=(
            jax.ShapeDtypeStruct((rows, width), bf),
            jax.ShapeDtypeStruct((rows, features), bf),
        ),
        in_specs=[any_spec] * 7,
        out_specs=(any_spec, vmem),
        scratch_shapes=[
            pltpu.VMEM((total, part), bf),
            pltpu.VMEM((16, 2, rows), jnp.int32),
            pltpu.VMEM((total, 128), jnp.int32),
            pltpu.VMEM((1024, part), bf),
            pltpu.VMEM((1024, part), bf),
            pltpu.VMEM((128, part), bf),
            pltpu.VMEM((part, features), bf),
            pltpu.VMEM((total, 128), f32),
            pltpu.VMEM((total, 128), f32),
            pltpu.VMEM((total, 128), f32),
            pltpu.VMEM((total, 128), f32),
            pltpu.VMEM((total, 128), f32),
            pltpu.VMEM((rows, 128), bf),
            pltpu.VMEM((total, 128), bf),
            pltpu.VMEM((total, 1024), bf),
            pltpu.VMEM((total, part), bf),
            pltpu.VMEM((total, features + 128), f32),
            pltpu.VMEM((total, features + 128), f32),
            pltpu.VMEM((total, features + 128), bf),
            pltpu.VMEM((total, features + 128), bf),
            pltpu.VMEM((1, part), f32),
        ]
        + [dma((n,)) for n in sems],
        compiler_params=pltpu.CompilerParams(
            collective_id=0, has_side_effects=True, vmem_limit_bytes=50 * 1024 * 1024
        ),
        cost_estimate=pl.CostEstimate(flops=6_000_000_000, bytes_accessed=20_000_000, transcendentals=0),
    )(
        *[
            pltpu.with_memory_space_constraint(a, pltpu.HBM)
            for a in (
                tokens,
                jnp.swapaxes(route_ids, 0, 1),
                jnp.swapaxes(adapter_down[0], 0, 1),
                adapter_up[0],
                jnp.swapaxes(router_weight, 0, 1),
                frozen_weight,
                norm_gain[None, :],
            )
        ]
    )


def solution(mesh):
    return jax.shard_map(
        shards,
        mesh=mesh,
        in_specs=(
            P(("fsdp", "adapter"), None),
            P(("fsdp", "adapter"), None),
            P(),
            P("adapter", None, None),
            P("adapter", None, None),
            P(),
            P("fsdp", None),
        ),
        out_specs=(P(("fsdp", "adapter"), None), P(("fsdp", "adapter"), None)),
        check_vma=False,
    )
```

```python
import functools

import jax
import jax.numpy as jnp
from jax import lax
from jax.experimental import pallas as pl
from jax.experimental.pallas import tpu as pltpu
from jax.sharding import PartitionSpec as P

MESH = pl.DeviceIdType.MESH
NX, NY, NZ = 8, 8, 8
CHUNK = 256


def mult(value, of):
    return pl.multiple_of(value, of)


def flip(bit, by):
    return bit + by * (1 - 2 * bit)


def kernel(
    tok, ids, down, up, router, frozen, gain, res, proj,
    X, IDS, CODE, DN, UP, RT, FZ, ACC0, ACC1, ACCR, P1, PIN, TS, TIN, A, RB, PB, PS, PO, PIN2, GAIN,
    tok_s, tok_r, id_s, id_r, xd_s, xd_r, xu_s, xu_r, yd_s, yd_r, yu_s, yu_r,
    fz_s, fz_r, p1_s, p1_r, t_s, t_r, rb_s, rb_r, ps_s, ps_r, p2_s, p2_r, rt_sem,
):
    half = tok.shape[0] // 2
    width = X.shape[1]
    total = X.shape[0]
    rank = down.shape[0]
    block = 4 * rank
    features = proj.shape[1]
    per_class = width // frozen.shape[0]
    fs, ad = lax.axis_index("fsdp"), lax.axis_index("adapter")
    x_lo = lax.div(fs, 2 * NZ)
    z = lax.rem(lax.div(fs, 2), NZ)
    core = lax.rem(fs, 2)
    x_hi = lax.div(ad, NY)
    y = lax.rem(ad, NY)
    x = 2 * x_hi + x_lo
    zb = lax.rem(z, 2)
    mine = x_lo * 4 + zb * 2 + core

    def dev(px, py, pz, pc):
        return (lax.rem(px, 2) * (2 * NZ) + pz * 2 + pc, lax.div(px, 2) * NY + py)

    def partner(h, d):
        px, pz, pc = x, z, core
        if d & 4:
            px = x + 1 - 2 * x_lo if h == 0 else lax.rem(x + NX - 1 + 2 * x_lo, NX)
        if d & 2:
            pz = z + 1 - 2 * zb if h == 0 else lax.rem(z + NZ - 1 + 2 * zb, NZ)
        if d & 1:
            pc = 1 - core
        return dev(px, y, pz, pc)

    def member(d):
        return flip(x_lo, (d >> 2) & 1) * 4 + flip(zb, (d >> 1) & 1) * 2 + flip(core, d & 1)

    def cols_of(m):
        return pl.ds(mult(m * width, 128), width)

    own_cols = cols_of(mine)
    x_groups = [(h, d) for d in (6, 4, 7, 5) for h in range(2)]
    z_groups = [(h, d) for d in (2, 3, 1) for h in range(2)]
    groups = x_groups + z_groups

    def remote(src, dst, send, recv, device):
        return pltpu.make_async_remote_copy(
            src_ref=src, dst_ref=dst, send_sem=send, recv_sem=recv, device_id=device, device_id_type=MESH
        )

    def rows_of(h, d):
        return pl.ds((h * 8 + d) * half, half)

    def tok_copy(h, d):
        i = h * 8 + d
        src = tok.at[pl.ds(h * half, half), cols_of(member(d))]
        return remote(src, X.at[rows_of(h, d)], tok_s.at[i], tok_r.at[i], partner(h, d))

    def id_copy(h, d):
        i = h * 8 + d
        return remote(ids, IDS.at[i], id_s.at[i], id_r.at[i], partner(h, d))

    def tok_local(h):
        cp = pltpu.make_async_copy(tok.at[pl.ds(h * half, half), own_cols], X.at[rows_of(h, 0)], tok_r.at[h * 8])
        cq = pltpu.make_async_copy(ids, IDS.at[h * 8], id_r.at[h * 8])
        return cp, cq

    def slot(py, px_hi):
        return pl.ds(mult(py * block + px_hi * rank, rank), rank)

    def x_copy(src, buf, send, recv, i):
        px = lax.rem(x + (2 * x_lo - 1) * i + NX, NX)
        cols = cols_of(lax.rem(px, 2) * 4 + zb * 2 + core)
        return remote(src.at[:, cols], buf.at[slot(y, x_hi)], send.at[i], recv.at[i], dev(px, y, z, core))

    def x_source(i):
        return lax.rem(x + (1 - 2 * x_lo) * (-i if i % 2 else i) + NX, NX)

    def x_local(src, buf, recv):
        return pltpu.make_async_copy(src.at[:, own_cols], buf.at[slot(y, x_hi)], recv.at[0])

    def steps(q, way):
        return 4 if (q < 2) == (way == 1) else 3

    def y_copy(buf, send, recv, q, way, s):
        origin = lax.rem(y + NY - way * (s - 1), NY)
        rows = slot(origin, lax.div(x_source(q), 2) if q else x_hi)
        device = dev(x, lax.rem(y + NY + way, NY), z, core)
        i = (q * 2 + (way + 1) // 2) * 4 + s - 1
        return remote(buf.at[rows], buf.at[rows], send.at[i], recv.at[i], device)

    def ring_start(buf, send, recv, q):
        for way in (1, -1):
            y_copy(buf, send, recv, q, way, 1).start()

    def ring_step(buf, send, recv, s):
        for q in range(4):
            for way in (1, -1):
                if s <= steps(q, way):
                    y_copy(buf, send, recv, q, way, s).wait_recv()
                    if s < steps(q, way):
                        y_copy(buf, send, recv, q, way, s + 1).start()

    fz_class = lax.div(fs, per_class)
    fz_core = lax.rem(fz_class, 2)
    fz_zb = lax.rem(lax.div(fz_class, 2), 2)
    fz_rows = frozen.shape[0]
    fz_slot = pl.ds(mult(lax.rem(fs, per_class) * fz_rows, 16), fz_rows)
    fz_self = fz_class == mine

    def fz_other(k):
        return jnp.logical_not(jnp.logical_and(2 * k + fz_zb == z, fz_core == core))

    def fz_copy(k):
        device = dev(x, y, 2 * k + fz_zb, fz_core)
        return remote(frozen, FZ.at[fz_slot], fz_s.at[k], fz_r.at[lax.rem(fs, per_class)], device)

    barrier = pltpu.get_barrier_semaphore()

    def greet(device):
        pl.semaphore_signal(barrier, inc=1, device_id=device, device_id_type=MESH)

    for i in range(1, 4):
        greet(dev(x_source(i), y, z, core))
    for way in (1, -1):
        greet(dev(x, lax.rem(y + NY + way, NY), z, core))
    for h, d in groups:
        greet(partner(h, d))
    for b in range(per_class):
        source = mine * per_class + b

        @pl.when(source != fs)
        def _():
            greet((source, ad))

    x_local(down, DN, xd_r).start()
    x_local(up, UP, xu_r).start()
    RT[...] = jnp.zeros_like(RT)
    rt_copy = pltpu.make_async_copy(router.at[:, own_cols], RT.at[pl.ds(2 * rank, rank)], rt_sem.at[0])
    rt_copy.start()
    gain_copy = pltpu.make_async_copy(gain.at[:, own_cols], GAIN, rt_sem.at[1])
    gain_copy.start()
    for h in range(2):
        for c in tok_local(h):
            c.start()
    pl.semaphore_wait(barrier, 14 + 3 + 2 + NZ // 2 - fz_self.astype(jnp.int32))

    for i in range(1, 4):
        x_copy(down, DN, xd_s, xd_r, i).start()
    x_local(down, DN, xd_r).wait()
    ring_start(DN, yd_s, yd_r, 0)
    for h, d in groups:
        id_copy(h, d).start()
    for h, d in z_groups:
        tok_copy(h, d).start()

    for i in range(1, 4):
        x_copy(down, DN, xd_s, xd_r, i).wait_recv()
        ring_start(DN, yd_s, yd_r, i)
    for h, d in x_groups:
        tok_copy(h, d).start()

    lane = lax.broadcasted_iota(jnp.int32, (CHUNK, 128), 1)
    group8 = (lane >> 5) * 8
    nt = (((1,), (1,)), ((), ()))

    def take_ids():
        for h in range(2):
            tok_local(h)[1].wait()
        for h, d in groups:
            id_copy(h, d).wait_recv()
        for h in range(2):
            for d in range(8):
                pair = IDS[h * 8 + d]
                both = (pair[0:1, :] * 32 + pair[1:2, :]).astype(jnp.float32)
                down_rows = jnp.transpose(jnp.broadcast_to(both, (128, 128)))
                CODE[rows_of(h, d), :] = down_rows[h * half : (h + 1) * half, :].astype(jnp.int32)

    def take_tokens():
        for h in range(2):
            tok_local(h)[0].wait()
        for h, d in z_groups + x_groups:
            tok_copy(h, d).wait_recv()
        rt_copy.wait()
        gain_copy.wait()

    def send_frozen():
        for k in range(NZ // 2):
            @pl.when(fz_other(k))
            def _():
                fz_copy(k).start()

        @pl.when(fz_self)
        def _():
            pltpu.make_async_copy(frozen, FZ.at[fz_slot], fz_r.at[lax.rem(fs, per_class)]).start()

    def low_rank(py, first=False):
        def body(i, carry):
            rows = pl.ds(mult(i * CHUNK, CHUNK), CHUNK)
            xs = X[rows, :]
            got = lax.dot_general(
                xs, DN[pl.ds(mult(py * block, block), block), :], nt, preferred_element_type=jnp.float32
            )
            c = CODE[rows, :]
            id0, id1 = c >> 5, c & 31
            named = group8 + py
            part0 = jnp.where(id0 == named, got, 0.0)
            part1 = jnp.where(id1 == named, got, 0.0)
            if first:
                ACC0[rows, :] = part0
                ACC1[rows, :] = part1
                logit = lax.dot_general(xs, RT[...], nt, preferred_element_type=jnp.float32)
                at = lane - 64
                ACCR[rows, :] = jnp.where(at == id0, logit, 0.0) - jnp.where(at == id1, logit, 0.0)
            else:
                ACC0[rows, :] += part0
                ACC1[rows, :] += part1
            return carry

        lax.fori_loop(0, total // CHUNK, body, 0)

    def low_rank_at(s):
        low_rank(lax.rem(y + NY - s, NY))
        if s < 4:
            low_rank(lax.rem(y + s, NY))

    def p1_copy(h, d):
        i = h * 8 + d
        return remote(P1.at[rows_of(h, d)], PIN.at[rows_of(h, d)], p1_s.at[i], p1_r.at[i], partner(h, d))

    def send_partials():
        def pack(i, carry):
            rows = pl.ds(mult(i * CHUNK, CHUNK), CHUNK)
            a0, a1 = ACC0[rows, :], ACC1[rows, :]
            a0 = a0 + pltpu.roll(a0, 64, 1)
            a0 = a0 + pltpu.roll(a0, 32, 1)
            a1 = a1 + pltpu.roll(a1, 64, 1)
            a1 = a1 + pltpu.roll(a1, 32, 1)
            low = jnp.where(lane < 32, a0, a1)
            P1[rows, :] = jnp.where(lane < 64, low, jnp.where(lane < 96, ACCR[rows, :], 0.0))
            return carry

        lax.fori_loop(0, total // CHUNK, pack, 0)
        for h, d in groups:
            p1_copy(h, d).start()

    def t_copy(h, d):
        i = h * 8 + d
        return remote(TS.at[pl.ds(h * half, half)], TIN.at[rows_of(h, d)], t_s.at[i], t_r.at[i], partner(h, d))

    def send_gated():
        lane_h = lax.broadcasted_iota(jnp.int32, (half, 128), 1)
        for h in range(2):
            for hh, d in groups:
                if hh == h:
                    p1_copy(h, d).wait_recv()
            s = P1[rows_of(h, 0), :]
            for d in range(1, 8):
                s = s + PIN[rows_of(h, d), :]
            rounded = s.astype(jnp.bfloat16).astype(jnp.float32)
            gap = jnp.sum(jnp.where(lane_h >= 64, s, 0.0), axis=1, keepdims=True)
            g0 = jax.nn.sigmoid(gap)
            gated = rounded * jnp.where(lane_h < 32, g0, 1.0 - g0)
            pair = jnp.where(lane_h < 64, gated, 0.0).astype(jnp.bfloat16)
            TS[pl.ds(h * half, half), :] = pair
            TIN[rows_of(h, 0), :] = pair
            for hh, d in groups:
                if hh == h:
                    t_copy(h, d).start()

    def take_gated():
        for h, d in groups:
            t_copy(h, d).wait_recv()

        def spread(i, carry):
            rows = pl.ds(mult(i * CHUNK, CHUNK), CHUNK)
            c = CODE[rows, :]
            id0, id1 = c >> 5, c & 31
            t = TIN[rows, :].astype(jnp.float32)
            t0 = jnp.where(lane < 32, t, 0.0)
            t1 = t - t0
            t0 = t0 + pltpu.roll(t0, 32, 1)
            t0 = t0 + pltpu.roll(t0, 64, 1)
            t1 = t1 + pltpu.roll(t1, 32, 1)
            t1 = t1 + pltpu.roll(t1, 64, 1)
            for py in range(NY):
                named = group8 + py
                part = jnp.where(id0 == named, t0, jnp.where(id1 == named, t1, 0.0))
                A[rows, py * block : (py + 1) * block] = part.astype(jnp.bfloat16)
            return carry

        lax.fori_loop(0, total // CHUNK, spread, 0)

    def down_step(s):
        ring_step(DN, yd_s, yd_r, s)

    def up_step(s):
        ring_step(UP, yu_s, yu_r, s)

    def up_send():
        for i in range(1, 4):
            x_copy(up, UP, xu_s, xu_r, i).start()

    def up_start():
        x_local(up, UP, xu_r).wait()
        ring_start(UP, yu_s, yu_r, 0)
        for i in range(1, 4):
            x_copy(up, UP, xu_s, xu_r, i).wait_recv()
            ring_start(UP, yu_s, yu_r, i)

    send_frozen()
    up_send()
    take_ids()
    down_step(1)
    down_step(2)
    take_tokens()
    low_rank(y, True)
    low_rank_at(1)
    down_step(3)
    up_start()
    low_rank_at(2)
    low_rank_at(3)
    down_step(4)
    low_rank_at(4)
    send_partials()
    up_step(1)
    send_gated()
    up_step(2)
    take_gated()
    up_step(3)
    up_step(4)
    for b in range(per_class):
        into = FZ.at[pl.ds(b * fz_rows, fz_rows)]
        pltpu.make_async_copy(frozen, into, fz_r.at[b]).wait()

    def rb_copy(h, d):
        i = h * 8 + d
        dst = res.at[pl.ds(h * half, half), own_cols]
        return remote(RB.at[rows_of(h, d)], dst, rb_s.at[i], rb_r.at[i], partner(h, d))

    def rb_local(h):
        dst = res.at[pl.ds(h * half, half), own_cols]
        return pltpu.make_async_copy(RB.at[rows_of(h, 0)], dst, rb_r.at[h * 8])

    def ps_copy(h, d):
        i = h * 8 + d
        return remote(PB.at[rows_of(h, d)], PS.at[rows_of(h, d - 1)], ps_s.at[i], ps_r.at[i], partner(0, 1))

    def p2_copy(h, d):
        i = h * 8 + d
        return remote(PO.at[rows_of(h, d)], PIN2.at[rows_of(h, d)], p2_s.at[i], p2_r.at[i], partner(h, d))

    for i in (1, 3, 0, 2):
        rows = pl.ds(i * CHUNK, CHUNK)
        delta = jnp.dot(A[rows, :], UP[...], preferred_element_type=jnp.float32)
        combined = X[rows, :].astype(jnp.float32) + delta
        RB[rows, :] = combined.astype(jnp.bfloat16)
        blocks = [(4 * i + k) for k in (2, 0, 3, 1)]
        for k in blocks:
            if k % 8:
                rb_copy(k // 8, k % 8).start()
            else:
                rb_local(k // 8).start()
        square = combined * combined
        lanes = square[:, 0:128]
        for j in range(1, width // 128):
            lanes = lanes + square[:, j * 128 : (j + 1) * 128]
        scaled = (combined * GAIN[...]).astype(jnp.bfloat16)
        PB[rows, 0:features] = jnp.dot(scaled, FZ[...], preferred_element_type=jnp.float32)
        PB[rows, features : features + 128] = lanes
        for k in blocks:
            if k % 2:
                ps_copy(k // 8, k % 8).start()

    for d in (6, 4, 2):
        for h in range(2):
            ps_copy(h, d + 1).wait_recv()
            rows = rows_of(h, d)
            PO[rows, :] = (PB[rows, :] + PS[rows, :]).astype(jnp.bfloat16)
            p2_copy(h, d).start()

    for h in range(2):
        rb_local(h).wait()
    for h, d in groups:
        rb_copy(h, d).wait_recv()
        for copy in (tok_copy, id_copy, p1_copy, t_copy, rb_copy):
            copy(h, d).wait_send()
    for h in range(2):
        for d in (1, 3, 5, 7):
            ps_copy(h, d).wait_send()
    for i in range(1, 4):
        x_copy(down, DN, xd_s, xd_r, i).wait_send()
        x_copy(up, UP, xu_s, xu_r, i).wait_send()
    for q in range(4):
        for way in (1, -1):
            for s in range(1, steps(q, way) + 1):
                y_copy(DN, yd_s, yd_r, q, way, s).wait_send()
                y_copy(UP, yu_s, yu_r, q, way, s).wait_send()
    for k in range(NZ // 2):
        @pl.when(fz_other(k))
        def _():
            fz_copy(k).wait_send()

    for h in range(2):
        ps_copy(h, 1).wait_recv()
        s = PB[rows_of(h, 0), :] + PS[rows_of(h, 0), :]
        for d in (6, 4, 2):
            p2_copy(h, d).wait_recv()
            s = s + PIN2[rows_of(h, d), :].astype(jnp.float32)
        mean = jnp.sum(s[:, features:], axis=1, keepdims=True) / tok.shape[1]
        proj[pl.ds(h * half, half), :] = (s[:, :features] * lax.rsqrt(mean + 1e-05)).astype(jnp.bfloat16)

    for h in range(2):
        for d in (2, 4, 6):
            p2_copy(h, d).wait_send()


def shards(tokens, route_ids, router_weight, adapter_down, adapter_up, norm_gain, frozen_weight):
    rows, width = tokens.shape
    part = width // 8
    features = frozen_weight.shape[1]
    total = 8 * rows
    bf, f32 = jnp.bfloat16, jnp.float32
    dma = pltpu.SemaphoreType.DMA
    any_spec = pl.BlockSpec(memory_space=pltpu.HBM)
    vmem = pl.BlockSpec(memory_space=pltpu.VMEM)
    sems = [16] * 4 + [4] * 4 + [32] * 4 + [4] * 2 + [16] * 10 + [2]
    return pl.pallas_call(
        kernel,
        out_shape=(
            jax.ShapeDtypeStruct((rows, width), bf),
            jax.ShapeDtypeStruct((rows, features), bf),
        ),
        in_specs=[any_spec] * 7,
        out_specs=(any_spec, vmem),
        scratch_shapes=[
            pltpu.VMEM((total, part), bf),
            pltpu.VMEM((16, 2, rows), jnp.int32),
            pltpu.VMEM((total, 128), jnp.int32),
            pltpu.VMEM((1024, part), bf),
            pltpu.VMEM((1024, part), bf),
            pltpu.VMEM((128, part), bf),
            pltpu.VMEM((part, features), bf),
            pltpu.VMEM((total, 128), f32),
            pltpu.VMEM((total, 128), f32),
            pltpu.VMEM((total, 128), f32),
            pltpu.VMEM((total, 128), f32),
            pltpu.VMEM((total, 128), f32),
            pltpu.VMEM((rows, 128), bf),
            pltpu.VMEM((total, 128), bf),
            pltpu.VMEM((total, 1024), bf),
            pltpu.VMEM((total, part), bf),
            pltpu.VMEM((total, features + 128), f32),
            pltpu.VMEM((total, features + 128), f32),
            pltpu.VMEM((total, features + 128), bf),
            pltpu.VMEM((total, features + 128), bf),
            pltpu.VMEM((1, part), f32),
        ]
        + [dma((n,)) for n in sems],
        compiler_params=pltpu.CompilerParams(
            collective_id=0, has_side_effects=True, vmem_limit_bytes=50 * 1024 * 1024
        ),
        cost_estimate=pl.CostEstimate(flops=6_000_000_000, bytes_accessed=20_000_000, transcendentals=0),
    )(
        *[
            pltpu.with_memory_space_constraint(a, pltpu.HBM)
            for a in (
                tokens,
                jnp.swapaxes(route_ids, 0, 1),
                jnp.swapaxes(adapter_down[0], 0, 1),
                adapter_up[0],
                jnp.swapaxes(router_weight, 0, 1),
                frozen_weight,
                norm_gain[None, :],
            )
        ]
    )


def solution(mesh):
    return jax.shard_map(
        shards,
        mesh=mesh,
        in_specs=(
            P(("fsdp", "adapter"), None),
            P(("fsdp", "adapter"), None),
            P(),
            P("adapter", None, None),
            P("adapter", None, None),
            P(),
            P("fsdp", None),
        ),
        out_specs=(P(("fsdp", "adapter"), None), P(("fsdp", "adapter"), None)),
        check_vma=False,
    )
```
